128 devices in a mesh: tm: 8 (over x_lo, z), patch: 16 (over x_hi, y, core).
Axes of the slice: x: 4 (x_hi: 2, x_lo: 2; x = x_hi * 2 + x_lo), y: 4, z: 4, core: 2. Of those that a mesh axis runs over, the one named last changes fastest.
Arguments:
- video_tokens: float32 [128, 256, 768], P('tm', 'patch'), may hold values from -6 to 6
- cotangent: float32 [128, 256, 768], P('tm', 'patch'), may hold values from -6 to 6
- weights: float32 [2, 768, 3072], replicated, may hold values from -0.21650635 to 0.21650635, as said below
Outputs:
- mixed: float32 [128, 256, 768], P('tm', 'patch')
- grad_input: float32 [128, 256, 768], P('tm', 'patch')
- grad_weights: float32 [2, 768, 3072], P(None, None, ('tm', 'patch'))
The draws below stay inside these ranges and needn't reach their ends.
Inputs may be any that keep to these rules, and one draw needn't show every extreme that they name: `weights`: entries scaled by 768 ** -0.5, one over the root of the fan-in.
All inputs are finite; a program needn't handle non-finite values.
Results may differ from the reference program's by a relative error of at most 0.0007.
Values sent between devices are 32-bit elements; how exact they have to be, the bound alone decides.
A program may use at most 192 MiB of HBM per device.

```python
import math
import jax
import jax.numpy as jnp
from jax import lax

D = 768
HEADS = 12
PATCHES = 256
FRAMES = 128
N_TM = 8
N_PATCH = 16


def draw_weights(key, part):
    key = jax.random.fold_in(key, 7)
    base_key = jax.random.fold_in(key, 0)
    scale = D ** (-0.5)
    result = jax.random.truncated_normal(base_key, -4.0, 4.0, (2, D, 4 * D), jnp.float32) * scale
    return result


def block_levels(stream_key, extent, shards, low, top_value):
    level = 1.0
    for dim, shards_of in shards:
        heights = jax.random.uniform(jax.random.fold_in(jax.random.fold_in(stream_key, 6), dim), (shards_of,), jnp.float32, low / len(shards), top_value / len(shards))
        level = level * jnp.repeat(jnp.exp(heights), extent[dim] // shards_of).reshape((-1,) + (1,) * (len(extent) - 1 - dim))
    return level


def noise(own_key, extent, scale, most, shards=(), dtype=jnp.bfloat16):
    factor_of = block_levels(own_key, extent, shards, -0.22, 0.18) if shards else 1.0
    drawn = jax.random.normal(own_key, extent, jnp.float32) * scale * factor_of
    return jnp.minimum(jnp.maximum(drawn, -most), most).astype(dtype)


def setup_inputs(seed: int = 0) -> dict:
    splits = jax.random.split(jax.random.key(seed), 4)
    return {
        "video_tokens": noise(splits[0], (FRAMES, PATCHES, D), 1.0, 6.0, ((0, 8), (1, 16)), jnp.float32),
        "cotangent": noise(splits[1], (FRAMES, PATCHES, D), 1.0, 6.0, ((0, 8), (1, 16)), jnp.float32),
        "weights": draw_weights(jax.random.fold_in(splits[3], 71), 0),
    }


HIGH = lax.Precision.HIGHEST

def normalize(inputs):
    center = inputs - lax.optimization_barrier(jnp.mean(inputs, axis=-1, keepdims=True))
    spread = lax.optimization_barrier(jnp.mean(center * center, axis=-1, keepdims=True))
    return center * lax.rsqrt(spread + 1e-05)

def attend(inputs, weight, layout_kind):
    width = inputs.shape[-1]
    head_dim = width // HEADS
    normed = normalize(inputs)
    project = jnp.einsum('abd,df->abf', normed, weight[:, :3 * width], precision=HIGH)
    shape = inputs.shape[:2] + (HEADS, head_dim)
    queries = project[..., :width].reshape(shape)
    keys_all = project[..., width:2 * width].reshape(shape)
    values = project[..., 2 * width:].reshape(shape)
    if layout_kind == 'lg':
        scores = jnp.einsum('lghe,mghe->ghlm', queries, keys_all, precision=HIGH)
    else:
        scores = jnp.einsum('glhe,gmhe->ghlm', queries, keys_all, precision=HIGH)
    scores = scores * (1.0 / math.sqrt(head_dim))
    row_max = lax.optimization_barrier(jnp.max(scores, axis=-1, keepdims=True))
    lifted = jnp.exp(scores - row_max)
    probs = lifted / lax.optimization_barrier(jnp.sum(lifted, axis=-1, keepdims=True))
    if layout_kind == 'lg':
        context = jnp.einsum('ghlm,mghe->lghe', probs, values, precision=HIGH)
    else:
        context = jnp.einsum('ghlm,gmhe->glhe', probs, values, precision=HIGH)
    merged = context.reshape(inputs.shape)
    return jnp.einsum('abd,df->abf', merged, weight[:, 3 * width:], precision=HIGH)

def reference(video_tokens, cotangent, weights):

    def forward(inputs, weight_set):
        frames, patches, width = inputs.shape
        blocks = inputs.reshape(frames, N_PATCH, patches // N_PATCH, width).transpose(1, 0, 2, 3)
        temporal = lax.map(lambda block: attend(block, weight_set[0], 'lg'), blocks)
        temporal = temporal.transpose(1, 0, 2, 3).reshape(inputs.shape)
        middle = inputs + temporal
        groups = middle.reshape(N_TM, frames // N_TM, patches, width)
        spatial = lax.map(lambda block: attend(block, weight_set[1], 'gl'), groups)
        return middle + spatial.reshape(inputs.shape)
    mixed, pullback = jax.vjp(forward, video_tokens, weights)
    grad_input, grad_raw = pullback(cotangent)
    factor = 1.0 / math.sqrt(video_tokens.shape[0] * video_tokens.shape[1])
    return (mixed, grad_input, grad_raw * factor)
```

```python
import math

import jax
import jax.numpy as jnp
from jax import lax
from jax.experimental import pallas as pl
from jax.experimental.pallas import tpu as pltpu
from jax.sharding import PartitionSpec as P

VMEM_LIMIT = 62 * 2**20
MESH = pl.DeviceIdType.MESH


def position():
    tm = lax.axis_index("tm")
    patch = lax.axis_index("patch")
    coords = (
        (patch // 8) * 2 + tm // 4,
        (patch // 2) % 4,
        tm % 4,
    )
    return tm, patch, patch % 2, coords


def flip(value, bits):
    result = value
    for bit in (1, 2, 4, 8):
        if bits & bit:
            has = (value // bit) % 2
            result = result + bit - 2 * bit * has
    return result


def partner(tm, patch, axis, mask):
    if axis == 0:
        return flip(tm, 4 * (mask & 1)), flip(patch, 8 * (mask >> 1))
    if axis == 1:
        return tm, flip(patch, 2 * mask)
    return flip(tm, mask), patch


class ScatterSum:
    def __init__(self, grads, core_in, ins, send, recv):
        self.grads, self.core_in, self.ins, self.send, self.recv = grads, core_in, ins, send, recv
        self.tm, self.patch, self.core, self.coords = position()

    def order(self, piece):
        turn = (piece // 2) % 3
        masks = (1, 3) if piece % 2 == 0 else (3, 1)
        return [(turn + k) % 3 for k in range(3)], masks

    def view(self, piece, stage, where):
        axes, _ = self.order(piece)
        index = [slice(None)] * 3
        for axis in axes[:stage]:
            index[axis] = self.coords[axis]
        index[axes[stage]] = where
        return self.grads.at[(self.core, piece) + tuple(index)]

    def core_copy(self, piece):
        return pltpu.make_async_remote_copy(
            src_ref=self.grads.at[1 - self.core, piece],
            dst_ref=self.core_in.at[piece],
            send_sem=self.send.at[piece, 0],
            recv_sem=self.recv.at[piece, 0],
            device_id=(self.tm, flip(self.patch, 1)),
            device_id_type=MESH,
        )

    def axis_copy(self, piece, stage, slot):
        axes, masks = self.order(piece)
        axis = axes[stage]
        here = self.coords[axis]
        where = (masks[0], 2, masks[1])[slot]
        mask = masks[1] if slot == 2 else masks[0]
        number = 1 + stage * 3 + slot
        return pltpu.make_async_remote_copy(
            src_ref=self.view(piece, stage, flip(here, where)),
            dst_ref=self.ins[stage].at[piece, slot],
            send_sem=self.send.at[piece, number],
            recv_sem=self.recv.at[piece, number],
            device_id=partner(self.tm, self.patch, axis, mask),
            device_id_type=MESH,
        )

    def steps(self):
        return 8

    def step(self, piece, number):
        if number == 0:
            self.core_copy(piece).start()
            return
        if number == 1:
            self.core_copy(piece).wait_recv()
            own = self.grads.at[self.core, piece]
            own[...] = own[...] + self.core_in[piece]
        else:
            stage, late = (number - 2) // 2, (number - 2) % 2
            axes, masks = self.order(piece)
            here = self.coords[axes[stage]]
            own = self.view(piece, stage, here)
            slots = self.ins[stage]
            if late == 0:
                self.axis_copy(piece, stage, 1).wait_recv()
                onward = self.view(piece, stage, flip(here, masks[1]))
                onward[...] = onward[...] + slots[piece, 1]
                self.axis_copy(piece, stage, 2).start()
                self.axis_copy(piece, stage, 0).wait_recv()
                own[...] = own[...] + slots[piece, 0]
                return
            self.axis_copy(piece, stage, 2).wait_recv()
            own[...] = own[...] + slots[piece, 2]
        stage = number // 2
        if stage < 3:
            self.axis_copy(piece, stage, 1).start()
            self.axis_copy(piece, stage, 0).start()

    def result(self, piece):
        x, y, z = self.coords
        return self.grads[self.core, piece, x, y, z]

    def finish(self, piece):
        self.core_copy(piece).wait_send()
        for stage in range(3):
            for slot in range(3):
                self.axis_copy(piece, stage, slot).wait_send()

    def neighbours(self):
        result = [(self.tm, flip(self.patch, 1))]
        for axis in range(3):
            for mask in (1, 3):
                result.append(partner(self.tm, self.patch, axis, mask))
        return result


F32, BF16 = jnp.float32, jnp.bfloat16
T = 256
D = 768
CHUNK = 256
CHUNKS = 3
SLOTS = 8
COLUMNS = 24
FACTOR = 1.0 / math.sqrt(128 * 256)
PIECES = 6


def split(value):
    high = value.astype(BF16)
    return high, (value - high.astype(F32)).astype(BF16)


def dot(a, b):
    return lax.dot_general(a, b, (((1,), (0,)), ((), ())), preferred_element_type=F32)


def dot_t(a, b):
    return lax.dot_general(a, b, (((1,), (1,)), ((), ())), preferred_element_type=F32)


def take(ref, c, rows):
    return jnp.concatenate([ref[2 * c, rows, :], ref[2 * c + 1, rows, :]], axis=1)


def put(ref, c, rows, value):
    ref[2 * c, rows, :] = value[:, :128]
    ref[2 * c + 1, rows, :] = value[:, 128:]


def regroup(src, dst, c):
    for lane in (2 * c, 2 * c + 1):
        for b in range(16):
            dst[lane, b * 16 : (b + 1) * 16, :] = src[lane, pl.ds(b, 16, stride=16), :]


def aligned(start, size, of):
    return pl.ds(pl.multiple_of(start, of), size)


def block_kernel(
    x_in, g_in, w_in, mixed_out, gi_out, gw_out,
    raw, l0, l1, xt, mid_home, mid_frame, gf, dmid_home, g_track, gi_home,
    staged, wh, wl, acts, spread, qn, kn, vn, qt, kt, probs, dt, do, dot_tr, bias,
    grads, core_in, in0, in1, in2,
    local_sem, stage_sem, tm_send, tm_recv, patch_send, patch_recv, rs_send, rs_recv, free_sem,
):
    tm, patch, core, coords = position()
    summing = ScatterSum(grads, core_in, (in0, in1, in2), rs_send, rs_recv)

    def tm_copy(src, dst, kind, c, d):
        other = flip(tm, d)
        return pltpu.make_async_remote_copy(
            src_ref=src.at[2 * c : 2 * c + 2, aligned(other * 32, 32, 32)],
            dst_ref=dst.at[2 * c : 2 * c + 2, aligned(tm * 32, 32, 32)],
            send_sem=tm_send.at[kind, c, d],
            recv_sem=tm_recv.at[kind, c, d],
            device_id=(other, patch),
            device_id_type=MESH,
        )

    def tm_start(src, dst, kind, c):
        for d in range(1, 8):
            tm_copy(src, dst, kind, c, d).start()
        own = aligned(tm * 32, 32, 32)
        for lane in (2 * c, 2 * c + 1):
            dst[lane, own, :] = src[lane, own, :]

    def tm_wait(src, dst, kind, c):
        for d in range(1, 8):
            tm_copy(src, dst, kind, c, d).wait_recv()

    def tm_sent(src, dst, kind, c):
        for d in range(1, 8):
            tm_copy(src, dst, kind, c, d).wait_send()

    def patch_copy(src, dst, kind, c, d):
        other = flip(patch, d)
        theirs, mine = aligned(other * 16, 16, 16), aligned(patch * 16, 16, 16)
        whole = len(src.shape) == 2
        return pltpu.make_async_remote_copy(
            src_ref=src.at[theirs] if whole else src.at[2 * c : 2 * c + 2, theirs],
            dst_ref=dst.at[mine] if whole else dst.at[2 * c : 2 * c + 2, mine],
            send_sem=patch_send.at[kind, c, d],
            recv_sem=patch_recv.at[kind, c, d],
            device_id=(tm, other),
            device_id_type=MESH,
        )

    def patch_start(src, dst, kind, c):
        for d in range(1, 16):
            patch_copy(src, dst, kind, c, d).start()
        if len(src.shape) == 3:
            own = aligned(patch * 16, 16, 16)
            for lane in (2 * c, 2 * c + 1):
                dst[lane, own, :] = src[lane, own, :]

    def patch_wait(src, dst, kind, c):
        for d in range(1, 16):
            patch_copy(src, dst, kind, c, d).wait_recv()

    def patch_sent(src, dst, kind, c):
        for d in range(1, 16):
            patch_copy(src, dst, kind, c, d).wait_send()

    def own_rows(src, dst, number):
        own = aligned(patch * 16, 16, 16)
        return pltpu.make_async_copy(src.at[own], dst.at[own], local_sem.at[number])

    def load(branch, k):
        slot = lax.rem(k, SLOTS)
        return pltpu.make_async_copy(
            w_in.at[branch, :, aligned(k * 128, 128, 128)], staged.at[slot], stage_sem.at[slot]
        )

    def prefetch(branch):
        for k in range(SLOTS):
            load(branch, k).start()

    def split_weights(branch, first, last):
        @pl.loop(first, last)
        def _(k):
            load(branch, k).wait()
            slot = lax.rem(k, SLOTS)
            lanes = aligned(k * 128, 128, 128)

            @pl.loop(0, 4)
            def _(r):
                rows = aligned(r * 192, 192, 64)
                high, low = split(staged[slot, rows, :])
                wh[rows, lanes] = high
                wl[rows, lanes] = low

            @pl.when(k + SLOTS < COLUMNS)
            def _():
                load(branch, k + SLOTS).start()

    def product(a, lanes):
        both = dot(a, wh[:, lanes])
        return both[:T] + both[T:] + dot(a[:T], wl[:, lanes])

    def normalize(branch, get):
        @pl.loop(0, 8)
        def _(r):
            rows = aligned(r * 32, 32, 32)
            parts = [get(c, rows) for c in range(CHUNKS)]
            total = parts[0] + parts[1] + parts[2]
            mean = jnp.sum(total, axis=1, keepdims=True) * (1.0 / D)
            parts = [part - mean for part in parts]
            square = parts[0] * parts[0] + parts[1] * parts[1] + parts[2] * parts[2]
            rstd = lax.rsqrt(jnp.sum(square, axis=1, keepdims=True) * (1.0 / D) + 1e-05)
            spread[branch, rows, :] = jnp.broadcast_to(rstd, (32, 128))
            for c in range(CHUNKS):
                high, low = split(parts[c] * rstd)
                acts[branch, 0, rows, c * CHUNK : (c + 1) * CHUNK] = high
                acts[branch, 0, aligned(T + r * 32, 32, 32), c * CHUNK : (c + 1) * CHUNK] = low

    def project(branch):
        normed = acts.at[branch, 0]

        def tile(i, base, scale):
            value = product(normed[...], aligned(base + i * 256, 256, 256))
            return value * scale if scale != 1.0 else value

        def natural(ref, lanes, value):
            high, low = split(value)
            ref[0:T, lanes] = high
            ref[T:, lanes] = low

        def turned(ref, i, value):
            high, low = split(value.T)
            rows = aligned(i * 256, 256, 256)
            ref[0, rows, :] = high
            ref[1, rows, :] = low

        @pl.loop(0, 3)
        def _(i):
            lanes = aligned(i * 256, 256, 256)
            value = tile(i, 0, 0.125)
            natural(qn, lanes, value)
            turned(qt.at[branch], i, value)

        @pl.loop(0, 3)
        def _(i):
            lanes = aligned(i * 256, 256, 256)
            value = tile(i, D, 1.0)
            natural(kn, lanes, value)
            turned(kt.at[branch], i, value)

        @pl.loop(0, 3)
        def _(i):
            natural(vn.at[branch], aligned(i * 256, 256, 256), tile(i, 2 * D, 1.0))

    def pair(ref, hp):
        lanes = aligned(hp * 128, 128, 128)
        return ref[0:T, lanes], ref[T:, lanes]

    def half_mask(e):
        lane = lax.broadcasted_iota(jnp.int32, (T, 128), 1)
        return jnp.where((lane >= 64) == (e == 1), 1.0, 0.0).astype(BF16)

    def inner(a, b, e):
        mask = half_mask(e)
        ah, al = a[0] * mask, a[1] * mask
        bh, bl = b
        return dot_t(
            jnp.concatenate([ah, al], axis=1), jnp.concatenate([bh, bh], axis=1)
        ) + dot_t(ah, bl)

    def probabilities(q, k, e, masked):
        scores = inner(q, k, e)
        if masked:
            scores = scores + bias[...]
        lifted = jnp.exp(scores - jnp.max(scores, axis=1, keepdims=True))
        return lifted * (1.0 / jnp.sum(lifted, axis=1, keepdims=True))

    def context(p, v):
        high, low = p
        both = dot(high, jnp.concatenate([v[0], v[1]], axis=1))
        return both[:, :128] + both[:, 128:] + dot(low, v[0])

    def store_context(branch, hp, values):
        lane = lax.broadcasted_iota(jnp.int32, (T, 128), 1)
        high, low = split(jnp.where(lane < 64, values[0], values[1]))
        lanes = aligned(hp * 128, 128, 128)
        acts[branch, 1, 0:T, lanes] = high
        acts[branch, 1, T:, lanes] = low

    def store_dt(start, value):
        high, low = split(value)
        rows = aligned(start, 64, 64)
        dt[0, rows, :] = high
        dt[1, rows, :] = low

    def head_back(branch, hp, e, p, ph, pw, v):
        dp = inner(pair(do, hp), v, e)
        ds = p * (dp - jnp.sum(dp * p, axis=1, keepdims=True))
        dsh, dsl = split(ds)
        start = hp * 128 + e * 64
        rows = aligned(start, 64, 64)

        def outer(ref, high, low, how):
            top = ref[0, rows, :]
            both = how(jnp.concatenate([top, ref[1, rows, :]], axis=0), high)
            return both[:64] + both[64:] + how(top, low)

        store_dt(start, outer(kt.at[branch], dsh, dsl, dot_t) * 0.125)
        store_dt(D + start, outer(qt.at[branch], dsh, dsl, dot))
        store_dt(2 * D + start, outer(dot_tr, ph, pw, dot))

    def out_gradient(get):
        for c in range(CHUNKS):
            value = get(c, slice(None))
            high, low = split(value)
            lanes = slice(c * CHUNK, (c + 1) * CHUNK)
            qn[0:T, lanes] = high
            qn[T:, lanes] = low
            high, low = split(value.T)
            rows = slice(3 * D + c * CHUNK, 3 * D + (c + 1) * CHUNK)
            dt[0, rows, :] = high
            dt[1, rows, :] = low

        @pl.loop(0, 3)
        def _(i):
            rows = aligned(i * 256, 256, 256)
            gh = qn[...]
            both = dot_t(gh, wh[rows, 3 * D :])
            value = both[:T] + both[T:] + dot_t(gh[:T], wl[rows, 3 * D :])
            high, low = split(value)
            do[0:T, rows] = high
            do[T:, rows] = low
            high, low = split(value.T)
            dot_tr[0, rows, :] = high
            dot_tr[1, rows, :] = low

    def back_to_normed():
        @pl.loop(0, CHUNKS)
        def _(c):
            rows = aligned(c * 256, 256, 256)
            value = (
                dot(wh[rows, : 3 * D], dt[0, : 3 * D, :])
                + dot(wh[rows, : 3 * D], dt[1, : 3 * D, :])
                + dot(wl[rows, : 3 * D], dt[0, : 3 * D, :])
            )
            put(l1, c, slice(None), value.T)

    def back_normalize(branch, get):
        @pl.loop(0, 8)
        def _(r):
            rows = aligned(r * 32, 32, 32)
            low_rows = aligned(T + r * 32, 32, 32)
            dn = [take(l1, c, rows) for c in range(CHUNKS)]
            n = [
                acts[branch, 0, rows, c * CHUNK : (c + 1) * CHUNK].astype(F32)
                + acts[branch, 0, low_rows, c * CHUNK : (c + 1) * CHUNK].astype(F32)
                for c in range(CHUNKS)
            ]
            mean = jnp.sum(dn[0] + dn[1] + dn[2], axis=1, keepdims=True) * (1.0 / D)
            along = dn[0] * n[0] + dn[1] * n[1] + dn[2] * n[2]
            along = jnp.sum(along, axis=1, keepdims=True) * (1.0 / D)
            rstd = spread[branch, rows, :][:, :1]
            for c in range(CHUNKS):
                put(l1, c, rows, get(c, rows) + rstd * (dn[c] - mean - n[c] * along))

    def weight_gradient(branch, c):
        lanes = slice(c * CHUNK, (c + 1) * CHUNK)

        @pl.loop(0, 4)
        def _(kind):
            rows = aligned(kind * D, D, D)
            source = kind // 3
            right_high = acts[branch, source, 0:T, lanes]
            right_low = acts[branch, source, T:, lanes]
            left = dt[0, rows, :]
            value = dot(left, right_high) + dot(left, right_low) + dot(dt[1, rows, :], right_high)
            for block in range(32):
                second, x_hi, y, half = block // 16, (block // 8) % 2, (block // 2) % 4, block % 2
                for lane in range(2):
                    grads[
                        half, 2 * c + lane, x_hi * 2 + kind // 2, y, 2 * lax.rem(kind, 2) + second
                    ] = value[block * 24 : block * 24 + 24, lane * 128 : (lane + 1) * 128]

    raw_loads = [
        pltpu.make_async_copy(
            x_in.at[:, lane * 128 : (lane + 1) * 128], raw.at[lane], local_sem.at[3 + lane]
        )
        for lane in range(2 * CHUNKS)
    ]
    for raw_load in raw_loads:
        raw_load.start()
    prefetch(0)
    g_own = own_rows(g_in, gf, 1)
    g_own.start()
    others = [(flip(tm, d), patch) for d in range(1, 8)]
    others += [(tm, flip(patch, d)) for d in range(1, 16)]
    others += [(flip(tm, 4), flip(patch, 8))]
    barrier = pltpu.get_barrier_semaphore()
    for other in others:
        pl.semaphore_signal(barrier, inc=1, device_id=other, device_id_type=MESH)
    row = (lax.broadcasted_iota(jnp.int32, (T, T), 0) // 16) % 2
    column = (lax.broadcasted_iota(jnp.int32, (T, T), 1) // 16) % 2
    bias[...] = jnp.where(row == column, 0.0, -1e30)
    for raw_load in raw_loads:
        raw_load.wait()
    for c in range(CHUNKS):
        regroup(raw, l0, c)
    pl.semaphore_wait(barrier, len(others))
    for c in range(CHUNKS):
        tm_start(l0, xt, 0, c)
    patch_start(g_in, gf, 0, 0)
    split_weights(0, 0, COLUMNS)
    prefetch(1)
    for c in range(CHUNKS):
        tm_wait(l0, xt, 0, c)

    normalize(0, lambda c, rows: take(xt, c, rows))
    project(0)

    @pl.loop(0, 6)
    def _(hp):
        q, k, v = pair(qn, hp), pair(kn, hp), pair(vn.at[0], hp)
        values = []
        for e in range(2):
            p = split(probabilities(q, k, e, True))
            probs[hp * 2 + e, 0] = p[0]
            probs[hp * 2 + e, 1] = p[1]
            values.append(context(p, v))
        store_context(0, hp, values)

    for c in range(CHUNKS):
        tm_sent(l0, xt, 0, c)
    for c in range(CHUNKS):
        value = product(acts[0, 1], pl.ds(3 * D + c * CHUNK, CHUNK))
        put(l1, c, slice(None), take(xt, c, slice(None)) + value)
        tm_start(l1, mid_home, 1, c)

    for c in range(CHUNKS):
        split_weights(1, c * 8, c * 8 + 8)
        tm_wait(l1, mid_home, 1, c)
        regroup(mid_home, l0, c)
        patch_start(l0, mid_frame, 1, c)
    prefetch(0)
    g_own.wait()
    patch_wait(g_in, gf, 0, 0)
    out_gradient(lambda c, rows: gf[rows, c * CHUNK : (c + 1) * CHUNK])
    for c in range(CHUNKS):
        patch_wait(l0, mid_frame, 1, c)

    normalize(1, lambda c, rows: take(mid_frame, c, rows))
    project(1)

    @pl.loop(0, 6)
    def _(hp):
        q, k, v = pair(qn, hp), pair(kn, hp), pair(vn.at[1], hp)
        values = []
        for e in range(2):
            p = probabilities(q, k, e, False)
            ph, pw = split(p)
            values.append(context((ph, pw), v))
            head_back(1, hp, e, p, ph, pw, v)
        store_context(1, hp, values)

    for c in range(CHUNKS):
        tm_sent(l1, mid_home, 1, c)
    back_to_normed()
    back_normalize(1, lambda c, rows: gf[rows, c * CHUNK : (c + 1) * CHUNK])
    for c in range(CHUNKS):
        patch_start(l1, dmid_home, 2, c)
    for c in range(CHUNKS):
        value = product(acts[1, 1], pl.ds(3 * D + c * CHUNK, CHUNK))
        gf[:, c * CHUNK : (c + 1) * CHUNK] = take(mid_frame, c, slice(None)) + value
    patch_start(gf, mixed_out, 3, 0)
    mixed_own = own_rows(gf, mixed_out, 2)
    mixed_own.start()

    for c in range(CHUNKS):
        patch_sent(l0, mid_frame, 1, c)
    for c in range(CHUNKS):
        weight_gradient(1, c)
        summing.step(2 * c, 0)
        summing.step(2 * c + 1, 0)
        patch_wait(l1, dmid_home, 2, c)
        regroup(dmid_home, l0, c)
        tm_start(l0, g_track, 2, c)
    def tick(number):
        for c in range(CHUNKS):
            if 1 <= number - c < summing.steps():
                for piece in (2 * c, 2 * c + 1):
                    summing.step(piece, number - c)

    split_weights(0, 0, 8)
    tick(1)
    split_weights(0, 8, 16)
    tick(2)
    split_weights(0, 16, 24)
    tick(3)
    for c in range(CHUNKS):
        tm_wait(l0, g_track, 2, c)

    out_gradient(lambda c, rows: take(g_track, c, rows))
    tick(4)

    def temporal_back(first, last):
        @pl.loop(first, last)
        def _(hp):
            v = pair(vn.at[0], hp)
            for e in range(2):
                ph, pw = probs[hp * 2 + e, 0], probs[hp * 2 + e, 1]
                head_back(0, hp, e, ph.astype(F32) + pw.astype(F32), ph, pw, v)

    temporal_back(0, 2)
    tick(5)
    temporal_back(2, 4)
    tick(6)
    temporal_back(4, 6)
    tick(7)
    tick(8)
    tick(9)
    for piece in range(PIECES):
        gw_out[1, :, piece * 128 : (piece + 1) * 128] = summing.result(piece) * FACTOR
        summing.finish(piece)
    for other in summing.neighbours():
        pl.semaphore_signal(free_sem, inc=1, device_id=other, device_id_type=MESH)
    for c in range(CHUNKS):
        weight_gradient(0, c)
        if c == 0:
            pl.semaphore_wait(free_sem, len(summing.neighbours()))
        summing.step(2 * c, 0)
        summing.step(2 * c + 1, 0)
    tick(1)
    for c in range(CHUNKS):
        patch_sent(l1, dmid_home, 2, c)
    back_to_normed()
    tick(2)
    back_normalize(0, lambda c, rows: take(g_track, c, rows))
    tick(3)
    for c in range(CHUNKS):
        tm_start(l1, gi_home, 3, c)
    tick(4)
    tick(5)
    for c in range(CHUNKS):
        tm_wait(l1, gi_home, 3, c)
        for lane in (2 * c, 2 * c + 1):
            for f in range(16):
                gi_out[f * 16 : (f + 1) * 16, lane * 128 : (lane + 1) * 128] = gi_home[
                    lane, pl.ds(f, 16, stride=16), :
                ]
    for number in range(6, 10):
        tick(number)
    for piece in range(PIECES):
        gw_out[0, :, piece * 128 : (piece + 1) * 128] = summing.result(piece) * FACTOR
        summing.finish(piece)

    patch_sent(g_in, gf, 0, 0)
    patch_sent(gf, mixed_out, 3, 0)
    patch_wait(gf, mixed_out, 3, 0)
    mixed_own.wait()
    for c in range(CHUNKS):
        tm_sent(l0, g_track, 2, c)
        tm_sent(l1, gi_home, 3, c)


def block(x, g, w):
    rows = pltpu.VMEM((T, D), F32)
    chunked = pltpu.VMEM((2 * CHUNKS, T, 128), F32)
    both = pltpu.VMEM((2 * T, D), BF16)
    turned = pltpu.VMEM((2, 2, D, T), BF16)
    scratch = dict(
        raw=chunked, l0=chunked, l1=chunked, xt=chunked, mid_home=chunked, mid_frame=chunked,
        gf=rows, dmid_home=chunked, g_track=chunked, gi_home=chunked,
        staged=pltpu.VMEM((SLOTS, D, 128), F32),
        wh=pltpu.VMEM((D, 4 * D), BF16),
        wl=pltpu.VMEM((D, 4 * D), BF16),
        acts=pltpu.VMEM((2, 2, 2 * T, D), BF16),
        spread=pltpu.VMEM((2, T, 128), F32),
        qn=both, kn=both,
        vn=pltpu.VMEM((2, 2 * T, D), BF16),
        qt=turned, kt=turned,
        probs=pltpu.VMEM((12, 2, T, T), BF16),
        dt=pltpu.VMEM((2, 4 * D, T), BF16),
        do=both,
        dot_tr=pltpu.VMEM((2, D, T), BF16),
        bias=pltpu.VMEM((T, T), F32),
        grads=pltpu.VMEM((2, PIECES, 4, 4, 4, 24, 128), F32),
        core_in=pltpu.VMEM((PIECES, 4, 4, 4, 24, 128), F32),
        in0=pltpu.VMEM((PIECES, 3, 4, 4, 24, 128), F32),
        in1=pltpu.VMEM((PIECES, 3, 4, 24, 128), F32),
        in2=pltpu.VMEM((PIECES, 3, 24, 128), F32),
        local_sem=pltpu.SemaphoreType.DMA((9,)),
        stage_sem=pltpu.SemaphoreType.DMA((SLOTS,)),
        tm_send=pltpu.SemaphoreType.DMA((4, 3, 8)),
        tm_recv=pltpu.SemaphoreType.DMA((4, 3, 8)),
        patch_send=pltpu.SemaphoreType.DMA((4, 3, 16)),
        patch_recv=pltpu.SemaphoreType.DMA((4, 3, 16)),
        rs_send=pltpu.SemaphoreType.DMA((PIECES, 10)),
        rs_recv=pltpu.SemaphoreType.DMA((PIECES, 10)),
        free_sem=pltpu.SemaphoreType.REGULAR,
    )
    anywhere = pl.BlockSpec(memory_space=pl.ANY)
    vmem = pl.BlockSpec(memory_space=pltpu.VMEM)
    return pl.pallas_call(
        block_kernel,
        out_shape=(
            jax.ShapeDtypeStruct((T, D), F32),
            jax.ShapeDtypeStruct((T, D), F32),
            jax.ShapeDtypeStruct((2, 24, D), F32),
        ),
        in_specs=[anywhere, anywhere, anywhere],
        out_specs=(anywhere, vmem, vmem),
        scratch_shapes=tuple(scratch.values()),
        compiler_params=pltpu.CompilerParams(
            collective_id=0, has_side_effects=True, vmem_limit_bytes=VMEM_LIMIT
        ),
    )(x, g, w)


def finish_kernel(*refs):
    copies = [pltpu.make_async_copy(refs[k], refs[3 + k], refs[6].at[k]) for k in range(3)]
    for copy in copies:
        copy.start()
    for copy in copies:
        copy.wait()


def finish(*results):
    anywhere = pl.BlockSpec(memory_space=pl.ANY)
    return pl.pallas_call(
        finish_kernel,
        out_shape=tuple(jax.ShapeDtypeStruct(r.shape, r.dtype) for r in results),
        in_specs=[anywhere] * 3,
        out_specs=(anywhere,) * 3,
        scratch_shapes=(pltpu.SemaphoreType.DMA((3,)),),
    )(*results)


def on_device(video_tokens, cotangent, weights):
    mixed, grad_input, summed = block(
        video_tokens.reshape(T, D), cotangent.reshape(T, D), weights
    )
    mixed, grad_input, grad_weights = finish(mixed, grad_input, summed)
    shape = video_tokens.shape
    return mixed.reshape(shape), grad_input.reshape(shape), grad_weights.transpose(0, 2, 1)


def solution(mesh):
    placed = (P("tm", "patch", None), P("tm", "patch", None), P())
    return jax.shard_map(
        on_device,
        mesh=mesh,
        in_specs=placed,
        out_specs=(P("tm", "patch", None), P("tm", "patch", None), P(None, None, ("tm", "patch"))),
        check_vma=False,
    )
```
